32 devices in a mesh: seq: 8 (over z, y), dp: 4 (over x, core).
Axes of the slice: x: 2, y: 2, z: 4, core: 2. Of those that a mesh axis runs over, the one named last changes fastest.
Arguments:
- queries: bfloat16 [4096, 20, 128], P(('dp', 'seq')), parts along dimension 0, may hold values from -6 to 6
- keys: bfloat16 [4096, 20, 128], P(('dp', 'seq')), parts along dimension 0, may hold values from -4 to 4
- values: bfloat16 [4096, 20, 128], P(('dp', 'seq')), parts along dimension 0, may hold values from -6 to 6
- out_grad: bfloat16 [4096, 20, 128], P(('dp', 'seq')), parts along dimension 0, may hold values from -96 to 96
- block_mask: int32 [20, 8, 5], replicated, may hold values from 0 to 1, as said below
Outputs:
- query_grad: bfloat16 [4096, 20, 128], P(('dp', 'seq')), parts along dimension 0
- key_grad: bfloat16 [4096, 20, 128], P(('dp', 'seq')), parts along dimension 0
- value_grad: bfloat16 [4096, 20, 128], P(('dp', 'seq')), parts along dimension 0
The draws below stay inside these ranges and needn't reach their ends.
There are 4 independent parts, one for each index of `dp`. The reference program is written for one: setup_inputs(seed, part) draws one part's arguments, and reference() takes and returns one part's arrays. A program takes and returns all parts, laid end to end along the dimension named above; an argument that names none is the same for every part. Nothing has to cross between parts.
Inputs may be any that keep to these rules, and one draw needn't show every extreme that they name: `block_mask`: entry j of row i names key block i + j - 2. The entry for j = 2 is always 1; entries naming blocks outside 0 to 7 are 0.
All inputs are finite; a program needn't handle non-finite values.
Results may differ from the reference program's by a relative error of at most 0.0075.
Values may be sent and summed in bfloat16 or wider, within the bound.
No kernel may reach another device: no remote copies, remote signals or barrier semaphores. Data moves between devices by JAX's collectives and lax.ppermute only.
A program may use at most 64 MiB of HBM per device.

```python
import math
import jax
import jax.numpy as jnp
from jax import lax

H = 20
E = 128
BLOCK = 128
RANGE = 2
BLOCKS = 8
TOKENS = 1024


def draw_queries(key, part):
    base_key = jax.random.fold_in(key, 1)
    return jax.random.truncated_normal(base_key, -4.0, 4.0, (TOKENS, H, E), jnp.float32).astype(jnp.bfloat16)


def draw_keys(key, part):
    base_key = jax.random.fold_in(key, 2)
    return jax.random.truncated_normal(base_key, -4.0, 4.0, (TOKENS, H, E), jnp.float32).astype(jnp.bfloat16)


def draw_block_mask(key, part):
    rate_key, bit_key = jax.random.split(jax.random.fold_in(key, 5))
    breadth = 2 * RANGE + 1
    keep_rates = jax.random.randint(rate_key, (H, BLOCKS // RANGE, 1, 1), 0, 1000)
    draw_bits = jax.random.randint(bit_key, (H, BLOCKS // RANGE, RANGE, breadth), 0, 1000)
    chosen = (draw_bits < keep_rates).reshape(H, BLOCKS, breadth)
    offsets = jnp.arange(breadth) - RANGE
    target = jnp.arange(BLOCKS)[:, None] + offsets[None, :]
    inside = (target >= 0) & (target < BLOCKS)
    allowed = chosen & inside[None] | (offsets == 0)[None, None, :]
    return allowed.astype(jnp.int32)


def block_scale(own_key, dims, pieces, low, top_value):
    factor_of, own = 1.0, jax.random.fold_in(own_key, 6)
    for axis_at, blocks in pieces:
        steps = jnp.exp(jax.random.uniform(jax.random.fold_in(own, axis_at), (blocks,), jnp.float32, low / len(pieces), top_value / len(pieces)))
        factor_of = factor_of * jnp.repeat(steps, dims[axis_at] // blocks).reshape([-1 if axis == axis_at else 1 for axis in range(len(dims))])
    return factor_of


def scatter_about(rng, extent, deviation, reach, cuts=(), kind=jnp.bfloat16):
    entries = jax.random.normal(rng, extent, jnp.float32) * deviation
    if len(cuts) > 0:
        entries = block_scale(rng, extent, cuts, -0.22, 0.18) * entries
    return jnp.clip(entries, min=-reach, max=reach).astype(kind)


def setup_inputs(seed: int = 0, part: int = 0) -> dict:
    key_of = jax.random.split(jax.random.key(seed), 6)
    own_keys = jax.random.split(jax.random.fold_in(key_of[5], part), 6)
    queries = draw_queries(jax.random.fold_in(jax.random.fold_in(key_of[5], part), 71), part)
    keys = draw_keys(jax.random.fold_in(jax.random.fold_in(key_of[5], part), 71), part)
    values = scatter_about(own_keys[2], (TOKENS, H, E), 1.0, 6.0, ((0, 8),))
    out_grad = scatter_about(own_keys[3], (TOKENS, H, E), 16.0, 96.0, ((0, 8),))
    block_mask = draw_block_mask(jax.random.fold_in(key_of[5], 71), part)
    return {"queries": queries, "keys": keys, "values": values, "out_grad": out_grad, "block_mask": block_mask}


def reference(queries, keys, values, out_grad, block_mask):
    token_count, head_count, head_width = queries.shape
    block_size = BLOCK
    reach_blocks = RANGE
    padding = reach_blocks * block_size
    window = (2 * reach_blocks + 1) * block_size
    score_scale = 1.0 / math.sqrt(head_width)
    queries_wide = queries.astype(jnp.float32)
    grad_wide = out_grad.astype(jnp.float32)
    key_padded = jnp.pad(keys.astype(jnp.float32), ((padding, padding), (0, 0), (0, 0)))
    value_padded = jnp.pad(values.astype(jnp.float32), ((padding, padding), (0, 0), (0, 0)))
    block_count = token_count // block_size

    def step_block(carry, block_index):
        key_acc, value_acc = carry
        first_row = block_index * block_size
        query_rows = lax.dynamic_slice_in_dim(queries_wide, first_row, block_size, 0)
        grad_rows = lax.dynamic_slice_in_dim(grad_wide, first_row, block_size, 0)
        key_window = lax.dynamic_slice_in_dim(key_padded, first_row, window, 0)
        value_window = lax.dynamic_slice_in_dim(value_padded, first_row, window, 0)
        mask_row = lax.dynamic_index_in_dim(block_mask, block_index, 1, False)
        allowed = jnp.repeat(mask_row > 0, block_size, axis=1)
        scores = jnp.einsum('qhe,khe->hqk', query_rows, key_window) * score_scale
        scores = jnp.where(allowed[:, None, :], scores, -jnp.inf)
        row_peak = lax.optimization_barrier(jnp.max(scores, axis=2, keepdims=True))
        exponents = jnp.exp(scores - row_peak)
        weights = exponents / lax.optimization_barrier(jnp.sum(exponents, axis=2, keepdims=True))
        weights_low = lax.optimization_barrier(weights.astype(jnp.bfloat16)).astype(jnp.float32)
        output = jnp.einsum('hqk,khe->qhe', weights_low, value_window)
        row_delta = lax.optimization_barrier(jnp.sum(grad_rows * output, axis=2))
        weight_grad = jnp.einsum('qhe,khe->hqk', grad_rows, value_window)
        score_grad = weights * (weight_grad - jnp.transpose(row_delta)[:, :, None])
        score_low = lax.optimization_barrier(score_grad.astype(jnp.bfloat16)).astype(jnp.float32)
        query_grad = score_scale * jnp.einsum('hqk,khe->qhe', score_low, key_window)
        key_part = score_scale * jnp.einsum('hqk,qhe->khe', score_low, query_rows)
        value_part = jnp.einsum('hqk,qhe->khe', weights_low, grad_rows)
        key_acc = lax.dynamic_update_slice_in_dim(key_acc, lax.dynamic_slice_in_dim(key_acc, first_row, window, 0) + key_part, first_row, 0)
        value_acc = lax.dynamic_update_slice_in_dim(value_acc, lax.dynamic_slice_in_dim(value_acc, first_row, window, 0) + value_part, first_row, 0)
        return ((key_acc, value_acc), query_grad.astype(jnp.bfloat16))
    initial = (jnp.zeros(key_padded.shape, jnp.float32), jnp.zeros(value_padded.shape, jnp.float32))
    (key_acc, value_acc), query_blocks = lax.scan(step_block, initial, jnp.arange(block_count, dtype=jnp.int32))
    query_grad = query_blocks.reshape(token_count, head_count, head_width)
    key_grad = key_acc[padding:padding + token_count].astype(jnp.bfloat16)
    value_grad = value_acc[padding:padding + token_count].astype(jnp.bfloat16)
    return (query_grad, key_grad, value_grad)
```

```python
from functools import partial
import math

import jax
import jax.numpy as jnp
from jax import lax
from jax.experimental import pallas as pl
from jax.experimental.pallas import tpu as pltpu
from jax.sharding import PartitionSpec as P

RANGE = 2
NEVER = -1e30
VMEM_BYTES = 40 * 2**20


def across(value, axis):
    size = lax.axis_size(axis)
    return lax.ppermute(value, axis, [(i, i ^ 1) for i in range(size)])


def partner_of(index, kind, range_total):
    other = index ^ 1 if kind == 0 else (index - 1 if index % 2 == 0 else index + 1)
    return other if 0 <= other < range_total else None


def beside(value, axis, kind):
    size = lax.axis_size(axis)
    pairs = []
    for i in range(size):
        other = partner_of(i // RANGE, kind, size // RANGE)
        if other is not None:
            pairs.append((i, other * RANGE + i % RANGE))
    return lax.ppermute(value, axis, pairs)


def nt(left, right):
    return lax.dot_general(left, right, (((1,), (1,)), ((), ())), preferred_element_type=jnp.float32)


def nn(left, right):
    return lax.dot_general(left, right, (((1,), (0,)), ((), ())), preferred_element_type=jnp.float32)


def tn(left, right):
    return lax.dot_general(left, right, (((0,), (0,)), ((), ())), preferred_element_type=jnp.float32)


def both(keep, other, head, which):
    return jnp.concatenate([keep[head, which], other[head, which]], axis=0)


def biased(scores, biases, block):
    rows = []
    for a in range(2):
        rows.append(
            jnp.concatenate(
                [
                    scores[a * block : (a + 1) * block, b * block : (b + 1) * block] + biases[a][b]
                    for b in range(2)
                ],
                axis=1,
            )
        )
    return jnp.concatenate(rows, axis=0)


def query_kernel(factor, scale, heads, table, qd_k, qd_o, *refs):
    key_refs, (dq_k, dq_o, stats) = refs[:6], refs[6:]
    block = qd_k.shape[2]
    first = pl.program_id(0) * heads
    for head in range(heads):
        queries = both(qd_k, qd_o, head, 0)
        grads = both(qd_k, qd_o, head, 1)
        scores = []
        for side in range(3):
            keys = both(key_refs[2 * side], key_refs[2 * side + 1], head, 0)
            at = (first + head) * 24 + side * 8
            biases = [[table[at + 2 * a + b] for b in range(2)] for a in range(2)]
            scores.append(biased(nt(keys, queries) * factor, biases, block))
        peak = jnp.max(jnp.maximum(jnp.maximum(scores[0], scores[1]), scores[2]), axis=0, keepdims=True)
        exps = [jnp.exp2(element - peak) for element in scores]
        total = jnp.sum(exps[0] + exps[1] + exps[2], axis=0, keepdims=True)
        weight_grads = [
            nt(both(key_refs[2 * side], key_refs[2 * side + 1], head, 1), grads) for side in range(3)
        ]
        mixed = exps[0] * weight_grads[0] + exps[1] * weight_grads[1] + exps[2] * weight_grads[2]
        inverse = 1.0 / total
        delta = jnp.sum(mixed, axis=0, keepdims=True) * inverse
        result = None
        for side in range(3):
            score_grad = (exps[side] * inverse * (weight_grads[side] - delta)).astype(jnp.bfloat16)
            term = tn(score_grad, both(key_refs[2 * side], key_refs[2 * side + 1], head, 0))
            result = term if result is None else result + term
        result = (result * scale).astype(jnp.bfloat16)
        dq_k[head] = result[:block]
        dq_o[head] = result[block:]
        stats[head, 0:1, :] = peak + jnp.log2(total)
        stats[head, 1:2, :] = delta


def key_kernel(factor, scale, heads, offset, table, kv_k, kv_o, *refs):
    query_refs, stat_refs, (dkv_k, dkv_o) = refs[:6], refs[6:9], refs[9:]
    block = kv_k.shape[2]
    first = pl.program_id(0) * heads + offset
    for head in range(heads):
        keys = both(kv_k, kv_o, head, 0)
        values = both(kv_k, kv_o, head, 1)
        key_grad = None
        value_grad = None
        for side in range(3):
            queries = both(query_refs[2 * side], query_refs[2 * side + 1], head, 0)
            grads = both(query_refs[2 * side], query_refs[2 * side + 1], head, 1)
            at = (first + head) * 24 + side * 8 + 4
            biases = [[table[at + 2 * a + b] for b in range(2)] for a in range(2)]
            level = stat_refs[side][head, 0:1, :]
            delta = stat_refs[side][head, 1:2, :]
            weights = jnp.exp2(biased(nt(keys, queries) * factor, biases, block) - level)
            weight_grad = nt(values, grads)
            score_grad = (weights * (weight_grad - delta)).astype(jnp.bfloat16)
            value_term = nn(weights.astype(jnp.bfloat16), grads)
            key_term = nn(score_grad, queries)
            value_grad = value_term if value_grad is None else value_grad + value_term
            key_grad = key_term if key_grad is None else key_grad + key_term
        key_grad = (key_grad * scale).astype(jnp.bfloat16)
        value_grad = value_grad.astype(jnp.bfloat16)
        dkv_k[head, 0] = key_grad[:block]
        dkv_o[head, 0] = key_grad[block:]
        dkv_k[head, 1] = value_grad[:block]
        dkv_o[head, 1] = value_grad[block:]


def bias_table(block_mask, heads, range_index, position, range_total):
    reach = (block_mask.shape[2] - 1) // 2
    even = range_index % 2 == 0
    ranges = jnp.stack(
        [range_index, range_index ^ 1, jnp.where(even, range_index - 1, range_index + 1)]
    )
    slots = jnp.stack([position, 1 - position])
    mine = range_index * RANGE + slots
    others = ranges[:, None] * RANGE + slots[None, :]
    shape = (3, 2, 2)
    key_first = jnp.broadcast_to(others[:, :, None], shape)
    query_first = jnp.broadcast_to(mine[None, None, :], shape)
    key_second = jnp.broadcast_to(mine[None, :, None], shape)
    query_second = jnp.broadcast_to(others[:, None, :], shape)
    key = jnp.stack([key_first, key_second], axis=1)
    query = jnp.stack([query_first, query_second], axis=1)
    total = range_total * RANGE
    inside = (key >= 0) & (key < total) & (query >= 0) & (query < total) & (abs(key - query) <= reach)
    picked = jax.nn.one_hot(query.reshape(-1), total, dtype=jnp.int32)[:, :, None] * (
        jax.nn.one_hot((key - query + reach).reshape(-1), 2 * reach + 1, dtype=jnp.int32)[:, None, :]
    )
    own = lax.dynamic_slice_in_dim(block_mask, position * heads, heads)
    found = jnp.sum(own[:, None] * picked[None], axis=(2, 3))
    allowed = (found > 0) & inside.reshape(-1)[None]
    return jnp.where(allowed, 0.0, NEVER).astype(jnp.float32).reshape(-1)


def per_device(queries, keys, values, out_grad, block_mask):
    block, head_count, width = queries.shape
    local = head_count // RANGE
    scale = 1.0 / math.sqrt(width)
    factor = scale * math.log2(math.e)
    device = lax.axis_index("seq")
    position = device % RANGE
    range_total = lax.axis_size("seq") // RANGE

    def by_head(left, right):
        return jnp.stack([jnp.transpose(left, (1, 0, 2)), jnp.transpose(right, (1, 0, 2))], axis=1)

    def half(pair, place):
        return lax.dynamic_slice_in_dim(pair, place * local, local)

    kv, qd = by_head(keys, values), by_head(queries, out_grad)
    kv_send, kv_keep = half(kv, 1 - position), half(kv, position)
    qd_send, qd_keep = half(qd, 1 - position), half(qd, position)
    kv_other = across(kv_send, "seq")
    kv_sides = [beside(kv_keep, "seq", 1), beside(kv_keep, "seq", 0)]
    qd_other = across(qd_send, "seq")
    kv_sides_other = [beside(kv_other, "seq", 1), beside(kv_other, "seq", 0)]
    qd_sides = [beside(qd_keep, "seq", 1), beside(qd_keep, "seq", 0)]
    qd_sides_other = [beside(qd_other, "seq", 1), beside(qd_other, "seq", 0)]
    table = bias_table(block_mask, local, device // RANGE, position, range_total)

    heads = 2 if local % 2 == 0 else 1
    pair_spec = pl.BlockSpec((heads, 2, block, width), lambda i: (i, 0, 0, 0))
    one_spec = pl.BlockSpec((heads, block, width), lambda i: (i, 0, 0))
    stat_spec = pl.BlockSpec((heads, 2, 2 * block), lambda i: (i, 0, 0))
    table_spec = pl.BlockSpec(memory_space=pltpu.SMEM)
    params = pltpu.CompilerParams(vmem_limit_bytes=VMEM_BYTES)
    tile = 4 * block * block * width

    dq_keep, dq_send, stats = pl.pallas_call(
        partial(query_kernel, factor, scale, heads),
        grid=(local // heads,),
        in_specs=[table_spec] + [pair_spec] * 8,
        out_specs=[one_spec, one_spec, stat_spec],
        out_shape=[
            jax.ShapeDtypeStruct((local, block, width), jnp.bfloat16),
            jax.ShapeDtypeStruct((local, block, width), jnp.bfloat16),
            jax.ShapeDtypeStruct((local, 2, 2 * block), jnp.float32),
        ],
        compiler_params=params,
        cost_estimate=pl.CostEstimate(
            flops=2 * 9 * local * tile, bytes_accessed=20 * local * block * width * 2, transcendentals=0
        ),
    )(
        table,
        qd_keep,
        qd_other,
        kv_keep,
        kv_other,
        kv_sides[1],
        kv_sides_other[1],
        kv_sides[0],
        kv_sides_other[0],
    )
    stat_sides = [beside(stats, "seq", 1), beside(stats, "seq", 0)]
    dq_back = across(dq_send, "seq")
    dkv_keep, dkv_send = pl.pallas_call(
        partial(key_kernel, factor, scale, heads, 0),
        grid=(local // heads,),
        in_specs=[table_spec] + [pair_spec] * 8 + [stat_spec] * 3,
        out_specs=[pair_spec, pair_spec],
        out_shape=[jax.ShapeDtypeStruct((local, 2, block, width), jnp.bfloat16)] * 2,
        compiler_params=params,
        cost_estimate=pl.CostEstimate(
            flops=2 * 12 * local * tile, bytes_accessed=20 * local * block * width * 2, transcendentals=0
        ),
    )(
        table,
        kv_keep,
        kv_other,
        qd_keep,
        qd_other,
        qd_sides[1],
        qd_sides_other[1],
        qd_sides[0],
        qd_sides_other[0],
        stats,
        stat_sides[1],
        stat_sides[0],
    )
    dkv_back = across(dkv_send, "seq")

    def home(mine, returned):
        low = jnp.where(position == 0, mine, returned)
        high = jnp.where(position == 0, returned, mine)
        return jnp.transpose(jnp.concatenate([low, high], axis=0), (1, 0, 2))

    return (
        home(dq_keep, dq_back),
        home(dkv_keep[:, 0], dkv_back[:, 0]),
        home(dkv_keep[:, 1], dkv_back[:, 1]),
    )


def solution(mesh):
    rows = P(("dp", "seq"), None, None)
    return jax.shard_map(
        per_device,
        mesh=mesh,
        in_specs=(rows, rows, rows, rows, P()),
        out_specs=(rows, rows, rows),
        check_vma=False,
    )
```

```python
from functools import partial
import math

import jax
import jax.numpy as jnp
from jax import lax
from jax.experimental import pallas as pl
from jax.experimental.pallas import tpu as pltpu
from jax.sharding import PartitionSpec as P

RANGE = 2
NEVER = -1e30
WORK = 8
VMEM_BYTES = 40 * 2**20


def cut_heads(local):
    step = (2 * local // 5 + 1) // 2 * 2
    return sorted({0, min(step, local), min(2 * step, local), local})


def across(value, axis):
    size = lax.axis_size(axis)
    return lax.ppermute(value, axis, [(i, i ^ 1) for i in range(size)])


def after(value, *earlier):
    return lax.optimization_barrier((value, *earlier))[0]


def partner_of(index, kind, range_total):
    other = index ^ 1 if kind == 0 else (index - 1 if index % 2 == 0 else index + 1)
    return other if 0 <= other < range_total else None


def beside(value, kind):
    size, clips = lax.axis_size("seq"), lax.axis_size("dp")
    pairs = []
    for i in range(size):
        other = partner_of(i // RANGE, kind, size // RANGE)
        for clip in range(clips):
            if other is not None:
                pairs.append((i * clips + clip, (other * RANGE + i % RANGE) * clips + clip))
            elif clips % 2 == 0:
                pairs.append((i * clips + clip, i * clips + (clip ^ 1)))
    return lax.ppermute(value, ("seq", "dp"), pairs)


def nt(left, right):
    return lax.dot_general(left, right, (((1,), (1,)), ((), ())), preferred_element_type=jnp.float32)


def nn(left, right):
    return lax.dot_general(left, right, (((1,), (0,)), ((), ())), preferred_element_type=jnp.float32)


def tn(left, right):
    return lax.dot_general(left, right, (((0,), (0,)), ((), ())), preferred_element_type=jnp.float32)


def both(keep, other, head, which):
    return jnp.concatenate([keep[head, which], other[head, which]], axis=0)


def biased(scores, biases, block):
    rows = []
    for a in range(2):
        rows.append(
            jnp.concatenate(
                [
                    scores[a * block : (a + 1) * block, b * block : (b + 1) * block] + biases[a][b]
                    for b in range(2)
                ],
                axis=1,
            )
        )
    return jnp.concatenate(rows, axis=0)


def query_kernel(factor, scale, heads, table, qd_k, qd_o, *refs):
    key_refs, (dq_k, dq_o, stats) = refs[:6], refs[6:]
    block = qd_k.shape[2]
    first = pl.program_id(0) * heads
    for head in range(heads):
        queries = both(qd_k, qd_o, head, 0)
        grads = both(qd_k, qd_o, head, 1)
        scores = []
        for side in range(3):
            keys = both(key_refs[2 * side], key_refs[2 * side + 1], head, 0)
            at = (first + head) * 24 + side * 8
            biases = [[table[at + 2 * a + b] for b in range(2)] for a in range(2)]
            scores.append(biased(nt(keys, queries) * factor, biases, block))
        peak = jnp.max(jnp.maximum(jnp.maximum(scores[0], scores[1]), scores[2]), axis=0, keepdims=True)
        exps = [jnp.exp2(element - peak) for element in scores]
        total = jnp.sum(exps[0] + exps[1] + exps[2], axis=0, keepdims=True)
        weight_grads = [
            nt(both(key_refs[2 * side], key_refs[2 * side + 1], head, 1), grads) for side in range(3)
        ]
        mixed = exps[0] * weight_grads[0] + exps[1] * weight_grads[1] + exps[2] * weight_grads[2]
        inverse = 1.0 / total
        delta = jnp.sum(mixed, axis=0, keepdims=True) * inverse
        result = None
        for side in range(3):
            score_grad = (exps[side] * inverse * (weight_grads[side] - delta)).astype(jnp.bfloat16)
            term = tn(score_grad, both(key_refs[2 * side], key_refs[2 * side + 1], head, 0))
            result = term if result is None else result + term
        result = (result * scale).astype(jnp.bfloat16)
        dq_k[head] = result[:block]
        dq_o[head] = result[block:]
        stats[head, 0:1, :] = peak + jnp.log2(total)
        stats[head, 1:2, :] = delta


def key_kernel(factor, scale, heads, offset, table, kv_k, kv_o, qd_k, qd_o, side_a, side_b, *refs):
    stat_refs, (dkv_k, dkv_o) = refs[:3], refs[3:]
    block = kv_k.shape[2]
    first = pl.program_id(0) * heads + offset
    for head in range(heads):
        keys = both(kv_k, kv_o, head, 0)
        values = both(kv_k, kv_o, head, 1)
        key_grad = None
        value_grad = None
        for side in range(3):
            if side == 0:
                queries, grads = both(qd_k, qd_o, head, 0), both(qd_k, qd_o, head, 1)
            else:
                ref = (side_a, side_b)[side - 1]
                queries = jnp.concatenate([ref[head, 0], ref[head, 2]], axis=0)
                grads = jnp.concatenate([ref[head, 1], ref[head, 3]], axis=0)
            at = (first + head) * 24 + side * 8 + 4
            biases = [[table[at + 2 * a + b] for b in range(2)] for a in range(2)]
            level = stat_refs[side][head, 0:1, :]
            delta = stat_refs[side][head, 1:2, :]
            weights = jnp.exp2(biased(nt(keys, queries) * factor, biases, block) - level)
            weight_grad = nt(values, grads)
            score_grad = (weights * (weight_grad - delta)).astype(jnp.bfloat16)
            value_term = nn(weights.astype(jnp.bfloat16), grads)
            key_term = nn(score_grad, queries)
            value_grad = value_term if value_grad is None else value_grad + value_term
            key_grad = key_term if key_grad is None else key_grad + key_term
        key_grad = (key_grad * scale).astype(jnp.bfloat16)
        value_grad = value_grad.astype(jnp.bfloat16)
        dkv_k[head, 0] = key_grad[:block]
        dkv_o[head, 0] = key_grad[block:]
        dkv_k[head, 1] = value_grad[:block]
        dkv_o[head, 1] = value_grad[block:]


def bias_table(block_mask, heads, range_index, position, range_total):
    reach = (block_mask.shape[2] - 1) // 2
    even = range_index % 2 == 0
    ranges = jnp.stack(
        [range_index, range_index ^ 1, jnp.where(even, range_index - 1, range_index + 1)]
    )
    slots = jnp.stack([position, 1 - position])
    mine = range_index * RANGE + slots
    others = ranges[:, None] * RANGE + slots[None, :]
    shape = (3, 2, 2)
    key_first = jnp.broadcast_to(others[:, :, None], shape)
    query_first = jnp.broadcast_to(mine[None, None, :], shape)
    key_second = jnp.broadcast_to(mine[None, :, None], shape)
    query_second = jnp.broadcast_to(others[:, None, :], shape)
    key = jnp.stack([key_first, key_second], axis=1)
    query = jnp.stack([query_first, query_second], axis=1)
    total = range_total * RANGE
    inside = (key >= 0) & (key < total) & (query >= 0) & (query < total) & (abs(key - query) <= reach)
    picked = jax.nn.one_hot(query.reshape(-1), total, dtype=jnp.int32)[:, :, None] * (
        jax.nn.one_hot((key - query + reach).reshape(-1), 2 * reach + 1, dtype=jnp.int32)[:, None, :]
    )
    own = lax.dynamic_slice_in_dim(block_mask, position * heads, heads)
    found = jnp.sum(own[:, None] * picked[None], axis=(2, 3))
    allowed = (found > 0) & inside.reshape(-1)[None]
    return jnp.where(allowed, 0.0, NEVER).astype(jnp.float32).reshape(-1)


def per_device(queries, keys, values, out_grad, block_mask):
    block, head_count, width = queries.shape
    local = head_count // RANGE
    scale = 1.0 / math.sqrt(width)
    factor = scale * math.log2(math.e)
    device = lax.axis_index("seq")
    position = device % RANGE
    range_total = lax.axis_size("seq") // RANGE

    def by_head(left, right):
        return jnp.stack([jnp.transpose(left, (1, 0, 2)), jnp.transpose(right, (1, 0, 2))], axis=1)

    def half(pair, place):
        return lax.dynamic_slice_in_dim(pair, place * local, local)

    kv, qd = by_head(keys, values), by_head(queries, out_grad)
    kv_send = half(kv, 1 - position)
    kv_keep = half(after(kv, kv_send), position)
    qd_send, qd_keep = half(qd, 1 - position), half(qd, position)
    kv_other = across(kv_send, "seq")
    kv_sides = [beside(kv_keep, 0), beside(kv_keep, 1)]
    qd_other = across(after(qd_send, kv_other), "seq")
    kv_sides_other = [beside(kv_other, 0), beside(kv_other, 1)]
    cuts = cut_heads(local)
    qd_pieces = [
        jnp.concatenate([qd_keep[low:high], qd_other[low:high]], axis=1) for low, high in zip(cuts, cuts[1:])
    ]
    qd_sides = [[beside(qd_pieces[0], 0), beside(qd_pieces[0], 1)]]
    table = bias_table(block_mask, local, device // RANGE, position, range_total)

    heads = 2 if local % 2 == 0 else 1
    pair_spec = pl.BlockSpec((heads, 2, block, width), lambda i: (i, 0, 0, 0))
    quad_spec = pl.BlockSpec((heads, 4, block, width), lambda i: (i, 0, 0, 0))
    one_spec = pl.BlockSpec((heads, block, width), lambda i: (i, 0, 0))
    stat_spec = pl.BlockSpec((heads, 2, 2 * block), lambda i: (i, 0, 0))
    table_spec = pl.BlockSpec(memory_space=pltpu.SMEM)
    params = pltpu.CompilerParams(vmem_limit_bytes=VMEM_BYTES)
    tile = 4 * block * block * width

    dq_keep, dq_send, stats = pl.pallas_call(
        partial(query_kernel, factor, scale, heads),
        grid=(local // heads,),
        in_specs=[table_spec] + [pair_spec] * 8,
        out_specs=[one_spec, one_spec, stat_spec],
        out_shape=[
            jax.ShapeDtypeStruct((local, block, width), jnp.bfloat16),
            jax.ShapeDtypeStruct((local, block, width), jnp.bfloat16),
            jax.ShapeDtypeStruct((local, 2, 2 * block), jnp.float32),
        ],
        compiler_params=params,
        cost_estimate=pl.CostEstimate(
            flops=WORK * 2 * 9 * local * tile, bytes_accessed=20 * local * block * width * 2, transcendentals=0
        ),
    )(
        table,
        qd_keep,
        qd_other,
        kv_keep,
        kv_other,
        kv_sides[0],
        kv_sides_other[0],
        kv_sides[1],
        kv_sides_other[1],
    )
    stat_sides = [beside(stats, 0), beside(stats, 1)]
    dq_back = across(after(dq_send, *stat_sides), "seq")
    dkv_keep, dkv_back = [], []
    for index, (low, high) in enumerate(zip(cuts, cuts[1:])):
        arrived = qd_sides[index]
        if index + 1 < len(qd_pieces):
            piece = after(qd_pieces[index + 1], qd_sides[-1][0])
            qd_sides.append([beside(piece, 0), beside(piece, 1)])
        count, shift = high - low, low // heads
        part_spec = pl.BlockSpec((heads, 2, block, width), lambda i, shift=shift: (i + shift, 0, 0, 0))
        stat_part = pl.BlockSpec((heads, 2, 2 * block), lambda i, shift=shift: (i + shift, 0, 0))
        keep, send = pl.pallas_call(
            partial(key_kernel, factor, scale, heads, low),
            grid=(count // heads,),
            in_specs=[table_spec] + [part_spec] * 4 + [quad_spec] * 2 + [stat_part] * 3,
            out_specs=[pair_spec, pair_spec],
            out_shape=[jax.ShapeDtypeStruct((count, 2, block, width), jnp.bfloat16)] * 2,
            compiler_params=params,
            cost_estimate=pl.CostEstimate(
                flops=WORK * 2 * 12 * count * tile, bytes_accessed=20 * count * block * width * 2, transcendentals=0
            ),
        )(
            table,
            kv_keep,
            kv_other,
            qd_keep,
            qd_other,
            *arrived,
            stats,
            *stat_sides,
        )
        dkv_keep.append(keep)
        dkv_back.append(across(send, "seq"))
    dkv_keep = jnp.concatenate(dkv_keep, axis=0)
    dkv_back = jnp.concatenate(dkv_back, axis=0)

    def home(mine, returned):
        low = jnp.where(position == 0, mine, returned)
        high = jnp.where(position == 0, returned, mine)
        return jnp.transpose(jnp.concatenate([low, high], axis=0), (1, 0, 2))

    return (
        home(dq_keep, dq_back),
        home(dkv_keep[:, 0], dkv_back[:, 0]),
        home(dkv_keep[:, 1], dkv_back[:, 1]),
    )


def solution(mesh):
    rows = P(("dp", "seq"), None, None)
    return jax.shard_map(
        per_device,
        mesh=mesh,
        in_specs=(rows, rows, rows, rows, P()),
        out_specs=(rows, rows, rows),
        check_vma=False,
    )
```

```python
from functools import partial
import math

import jax
import jax.numpy as jnp
from jax import lax
from jax.experimental import pallas as pl
from jax.experimental.pallas import tpu as pltpu
from jax.sharding import PartitionSpec as P

RANGE = 2
NEVER = -1e30
WORK = 8
VMEM_BYTES = 40 * 2**20


def cut_heads(local):
    step = (2 * local // 5 + 1) // 2 * 2
    return sorted({0, min(step, local), min(2 * step, local), local})


def across(value, axis):
    size = lax.axis_size(axis)
    return lax.ppermute(value, axis, [(i, i ^ 1) for i in range(size)])


def after(value, *earlier):
    return lax.optimization_barrier((value, *earlier))[0]


def partner_of(index, kind, range_total):
    other = index ^ 1 if kind == 0 else (index - 1 if index % 2 == 0 else index + 1)
    return other if 0 <= other < range_total else None


def beside(value, kind):
    size, clips = lax.axis_size("seq"), lax.axis_size("dp")
    pairs = []
    for i in range(size):
        other = partner_of(i // RANGE, kind, size // RANGE)
        for clip in range(clips):
            if other is not None:
                pairs.append((i * clips + clip, (other * RANGE + i % RANGE) * clips + clip))
            elif clips % 2 == 0:
                pairs.append((i * clips + clip, i * clips + (clip ^ 1)))
    return lax.ppermute(value, ("seq", "dp"), pairs)


def nt(left, right):
    return lax.dot_general(left, right, (((1,), (1,)), ((), ())), preferred_element_type=jnp.float32)


def nn(left, right):
    return lax.dot_general(left, right, (((1,), (0,)), ((), ())), preferred_element_type=jnp.float32)


def tn(left, right):
    return lax.dot_general(left, right, (((0,), (0,)), ((), ())), preferred_element_type=jnp.float32)


def both(keep, other, head, which):
    return jnp.concatenate([keep[head, which], other[head, which]], axis=0)


def biased(scores, biases, block):
    rows = []
    for a in range(2):
        rows.append(
            jnp.concatenate(
                [
                    scores[a * block : (a + 1) * block, b * block : (b + 1) * block] + biases[a][b]
                    for b in range(2)
                ],
                axis=1,
            )
        )
    return jnp.concatenate(rows, axis=0)


def query_kernel(factor, scale, heads, table, qd_k, qd_o, *refs):
    key_refs, (dq_k, dq_o, stats) = refs[:6], refs[6:]
    block = qd_k.shape[2]
    first = pl.program_id(0) * heads
    for head in range(heads):
        queries = both(qd_k, qd_o, head, 0)
        grads = both(qd_k, qd_o, head, 1)
        scores = []
        for side in range(3):
            keys = both(key_refs[2 * side], key_refs[2 * side + 1], head, 0)
            at = (first + head) * 24 + side * 8
            biases = [[table[at + 2 * a + b] for b in range(2)] for a in range(2)]
            scores.append(biased(nt(keys, queries) * factor, biases, block))
        peak = jnp.max(jnp.maximum(jnp.maximum(scores[0], scores[1]), scores[2]), axis=0, keepdims=True)
        exps = [jnp.exp2(element - peak) for element in scores]
        total = jnp.sum(exps[0] + exps[1] + exps[2], axis=0, keepdims=True)
        weight_grads = [
            nt(both(key_refs[2 * side], key_refs[2 * side + 1], head, 1), grads) for side in range(3)
        ]
        mixed = exps[0] * weight_grads[0] + exps[1] * weight_grads[1] + exps[2] * weight_grads[2]
        inverse = 1.0 / total
        delta = jnp.sum(mixed, axis=0, keepdims=True) * inverse
        result = None
        for side in range(3):
            score_grad = (exps[side] * inverse * (weight_grads[side] - delta)).astype(jnp.bfloat16)
            term = tn(score_grad, both(key_refs[2 * side], key_refs[2 * side + 1], head, 0))
            result = term if result is None else result + term
        result = (result * scale).astype(jnp.bfloat16)
        dq_k[head] = result[:block]
        dq_o[head] = result[block:]
        stats[head, 0:1, :] = peak + jnp.log2(total)
        stats[head, 1:2, :] = delta


def key_kernel(factor, scale, heads, offset, table, kv_k, kv_o, qd_k, qd_o, side_a, side_b, *refs):
    stat_refs, (dkv_k, dkv_o) = refs[:3], refs[3:]
    block = kv_k.shape[2]
    first = pl.program_id(0) * heads + offset
    for head in range(heads):
        keys = both(kv_k, kv_o, head, 0)
        values = both(kv_k, kv_o, head, 1)
        key_grad = None
        value_grad = None
        for side in range(3):
            if side == 0:
                queries, grads = both(qd_k, qd_o, head, 0), both(qd_k, qd_o, head, 1)
            else:
                ref = (side_a, side_b)[side - 1]
                queries = jnp.concatenate([ref[head, 0], ref[head, 2]], axis=0)
                grads = jnp.concatenate([ref[head, 1], ref[head, 3]], axis=0)
            at = (first + head) * 24 + side * 8 + 4
            biases = [[table[at + 2 * a + b] for b in range(2)] for a in range(2)]
            level = stat_refs[side][head, 0:1, :]
            delta = stat_refs[side][head, 1:2, :]
            weights = jnp.exp2(biased(nt(keys, queries) * factor, biases, block) - level)
            weight_grad = nt(values, grads)
            score_grad = (weights * (weight_grad - delta)).astype(jnp.bfloat16)
            value_term = nn(weights.astype(jnp.bfloat16), grads)
            key_term = nn(score_grad, queries)
            value_grad = value_term if value_grad is None else value_grad + value_term
            key_grad = key_term if key_grad is None else key_grad + key_term
        key_grad = (key_grad * scale).astype(jnp.bfloat16)
        value_grad = value_grad.astype(jnp.bfloat16)
        dkv_k[head, 0] = key_grad[:block]
        dkv_o[head, 0] = key_grad[block:]
        dkv_k[head, 1] = value_grad[:block]
        dkv_o[head, 1] = value_grad[block:]


def bias_table(block_mask, heads, range_index, position, range_total):
    reach = (block_mask.shape[2] - 1) // 2
    even = range_index % 2 == 0
    ranges = jnp.stack(
        [range_index, range_index ^ 1, jnp.where(even, range_index - 1, range_index + 1)]
    )
    slots = jnp.stack([position, 1 - position])
    mine = range_index * RANGE + slots
    others = ranges[:, None] * RANGE + slots[None, :]
    shape = (3, 2, 2)
    key_first = jnp.broadcast_to(others[:, :, None], shape)
    query_first = jnp.broadcast_to(mine[None, None, :], shape)
    key_second = jnp.broadcast_to(mine[None, :, None], shape)
    query_second = jnp.broadcast_to(others[:, None, :], shape)
    key = jnp.stack([key_first, key_second], axis=1)
    query = jnp.stack([query_first, query_second], axis=1)
    total = range_total * RANGE
    inside = (key >= 0) & (key < total) & (query >= 0) & (query < total) & (abs(key - query) <= reach)
    picked = jax.nn.one_hot(query.reshape(-1), total, dtype=jnp.int32)[:, :, None] * (
        jax.nn.one_hot((key - query + reach).reshape(-1), 2 * reach + 1, dtype=jnp.int32)[:, None, :]
    )
    own = lax.dynamic_slice_in_dim(block_mask, position * heads, heads)
    found = jnp.sum(own[:, None] * picked[None], axis=(2, 3))
    allowed = (found > 0) & inside.reshape(-1)[None]
    return jnp.where(allowed, 0.0, NEVER).astype(jnp.float32).reshape(-1)


def per_device(queries, keys, values, out_grad, block_mask):
    block, head_count, width = queries.shape
    local = head_count // RANGE
    scale = 1.0 / math.sqrt(width)
    factor = scale * math.log2(math.e)
    device = lax.axis_index("seq")
    position = device % RANGE
    range_total = lax.axis_size("seq") // RANGE

    def by_head(left, right):
        return jnp.stack([jnp.transpose(left, (1, 0, 2)), jnp.transpose(right, (1, 0, 2))], axis=1)

    def half(pair, place):
        return lax.dynamic_slice_in_dim(pair, place * local, local)

    kv, qd = by_head(keys, values), by_head(queries, out_grad)
    kv_send = half(kv, 1 - position)
    kv_keep = half(after(kv, kv_send), position)
    qd_send, qd_keep = half(qd, 1 - position), half(qd, position)
    kv_other = across(kv_send, "seq")
    kv_sides = [beside(kv_keep, 0), beside(kv_keep, 1)]
    qd_other = across(after(qd_send, kv_other), "seq")
    kv_sides_other = [beside(kv_other, 0), beside(kv_other, 1)]
    cuts = cut_heads(local)
    qd_pieces = [
        jnp.concatenate([qd_keep[low:high], qd_other[low:high]], axis=1) for low, high in zip(cuts, cuts[1:])
    ]
    qd_sides = [[beside(qd_pieces[0], 0), beside(qd_pieces[0], 1)]]
    table = bias_table(block_mask, local, device // RANGE, position, range_total)

    heads = 2 if local % 2 == 0 else 1
    pair_spec = pl.BlockSpec((heads, 2, block, width), lambda i: (i, 0, 0, 0))
    quad_spec = pl.BlockSpec((heads, 4, block, width), lambda i: (i, 0, 0, 0))
    one_spec = pl.BlockSpec((heads, block, width), lambda i: (i, 0, 0))
    stat_spec = pl.BlockSpec((heads, 2, 2 * block), lambda i: (i, 0, 0))
    table_spec = pl.BlockSpec(memory_space=pltpu.SMEM)
    params = pltpu.CompilerParams(vmem_limit_bytes=VMEM_BYTES)
    tile = 4 * block * block * width

    dq_keep, dq_send, stats = pl.pallas_call(
        partial(query_kernel, factor, scale, heads),
        grid=(local // heads,),
        in_specs=[table_spec] + [pair_spec] * 8,
        out_specs=[one_spec, one_spec, stat_spec],
        out_shape=[
            jax.ShapeDtypeStruct((local, block, width), jnp.bfloat16),
            jax.ShapeDtypeStruct((local, block, width), jnp.bfloat16),
            jax.ShapeDtypeStruct((local, 2, 2 * block), jnp.float32),
        ],
        compiler_params=params,
        cost_estimate=pl.CostEstimate(
            flops=WORK * 2 * 9 * local * tile, bytes_accessed=20 * local * block * width * 2, transcendentals=0
        ),
    )(
        table,
        qd_keep,
        qd_other,
        kv_keep,
        kv_other,
        kv_sides[0],
        kv_sides_other[0],
        kv_sides[1],
        kv_sides_other[1],
    )
    stats = after(stats, qd_sides[0][0])
    stat_sides = [beside(stats, 0), beside(stats, 1)]
    dq_back = across(dq_send, "seq")
    dkv_keep, dkv_back = [], []
    for index, (low, high) in enumerate(zip(cuts, cuts[1:])):
        arrived = qd_sides[index]
        if index + 1 < len(qd_pieces):
            piece = after(qd_pieces[index + 1], qd_sides[-1][0] if index == 0 else dkv_back[0])
            qd_sides.append([beside(piece, 0), beside(piece, 1)])
        count = high - low
        heads = 2 if low % 2 == 0 and count % 2 == 0 else 1
        shift = low // heads
        pair_spec = pl.BlockSpec((heads, 2, block, width), lambda i: (i, 0, 0, 0))
        quad_spec = pl.BlockSpec((heads, 4, block, width), lambda i: (i, 0, 0, 0))
        part_spec = pl.BlockSpec((heads, 2, block, width), lambda i, shift=shift: (i + shift, 0, 0, 0))
        stat_part = pl.BlockSpec((heads, 2, 2 * block), lambda i, shift=shift: (i + shift, 0, 0))
        keep, send = pl.pallas_call(
            partial(key_kernel, factor, scale, heads, low),
            grid=(count // heads,),
            in_specs=[table_spec] + [part_spec] * 4 + [quad_spec] * 2 + [stat_part] * 3,
            out_specs=[pair_spec, pair_spec],
            out_shape=[jax.ShapeDtypeStruct((count, 2, block, width), jnp.bfloat16)] * 2,
            compiler_params=params,
            cost_estimate=pl.CostEstimate(
                flops=WORK * 2 * 12 * count * tile, bytes_accessed=20 * count * block * width * 2, transcendentals=0
            ),
        )(
            table,
            kv_keep,
            kv_other,
            qd_keep,
            qd_other,
            *arrived,
            stats,
            *stat_sides,
        )
        dkv_keep.append(keep)
        dkv_back.append(across(send, "seq"))
    dkv_keep = jnp.concatenate(dkv_keep, axis=0)
    dkv_back = jnp.concatenate(dkv_back, axis=0)

    def home(mine, returned):
        low = jnp.where(position == 0, mine, returned)
        high = jnp.where(position == 0, returned, mine)
        return jnp.transpose(jnp.concatenate([low, high], axis=0), (1, 0, 2))

    return (
        home(dq_keep, dq_back),
        home(dkv_keep[:, 0], dkv_back[:, 0]),
        home(dkv_keep[:, 1], dkv_back[:, 1]),
    )


def solution(mesh):
    rows = P(("dp", "seq"), None, None)
    return jax.shard_map(
        per_device,
        mesh=mesh,
        in_specs=(rows, rows, rows, rows, P()),
        out_specs=(rows, rows, rows),
        check_vma=False,
    )
```

```python
from functools import partial
import math

import jax
import jax.numpy as jnp
from jax import lax
from jax.experimental import pallas as pl
from jax.experimental.pallas import tpu as pltpu
from jax.sharding import PartitionSpec as P

RANGE = 2
NEVER = -1e30
WORK = 8
VMEM_BYTES = 40 * 2**20


def cut_heads(local):
    step = (2 * local // 5 + 1) // 2 * 2
    return sorted({0, min(step, local), min(2 * step, local), local})


def across(value, axis):
    size = lax.axis_size(axis)
    return lax.ppermute(value, axis, [(i, i ^ 1) for i in range(size)])


def after(value, *earlier):
    return lax.optimization_barrier((value, *earlier))[0]


def partner_of(index, kind, range_total):
    other = index ^ 1 if kind == 0 else (index - 1 if index % 2 == 0 else index + 1)
    return other if 0 <= other < range_total else None


def beside(value, kind):
    size, clips = lax.axis_size("seq"), lax.axis_size("dp")
    pairs = []
    for i in range(size):
        other = partner_of(i // RANGE, kind, size // RANGE)
        for clip in range(clips):
            if other is not None:
                pairs.append((i * clips + clip, (other * RANGE + i % RANGE) * clips + clip))
            elif clips % 2 == 0:
                pairs.append((i * clips + clip, i * clips + (clip ^ 1)))
    return lax.ppermute(value, ("seq", "dp"), pairs)


def nt(left, right):
    return lax.dot_general(left, right, (((1,), (1,)), ((), ())), preferred_element_type=jnp.float32)


def nn(left, right):
    return lax.dot_general(left, right, (((1,), (0,)), ((), ())), preferred_element_type=jnp.float32)


def tn(left, right):
    return lax.dot_general(left, right, (((0,), (0,)), ((), ())), preferred_element_type=jnp.float32)


def both(keep, other, head, which):
    return jnp.concatenate([keep[head, which], other[head, which]], axis=0)


def biased(scores, biases, block):
    rows = []
    for a in range(2):
        rows.append(
            jnp.concatenate(
                [
                    scores[a * block : (a + 1) * block, b * block : (b + 1) * block] + biases[a][b]
                    for b in range(2)
                ],
                axis=1,
            )
        )
    return jnp.concatenate(rows, axis=0)


def query_kernel(factor, scale, heads, table, qd_k, qd_o, *refs):
    key_refs, (dq_k, dq_o, stats) = refs[:6], refs[6:]
    block = qd_k.shape[2]
    first = pl.program_id(0) * heads
    for head in range(heads):
        queries = both(qd_k, qd_o, head, 0)
        grads = both(qd_k, qd_o, head, 1)
        scores = []
        for side in range(3):
            keys = both(key_refs[2 * side], key_refs[2 * side + 1], head, 0)
            at = (first + head) * 24 + side * 8
            biases = [[table[at + 2 * a + b] for b in range(2)] for a in range(2)]
            scores.append(biased(nt(keys, queries) * factor, biases, block))
        peak = jnp.max(jnp.maximum(jnp.maximum(scores[0], scores[1]), scores[2]), axis=0, keepdims=True)
        exps = [jnp.exp2(element - peak) for element in scores]
        total = jnp.sum(exps[0] + exps[1] + exps[2], axis=0, keepdims=True)
        weight_grads = [
            nt(both(key_refs[2 * side], key_refs[2 * side + 1], head, 1), grads) for side in range(3)
        ]
        inverse = 1.0 / total
        weights = [element * inverse for element in exps]
        mixed = [
            weight.astype(jnp.bfloat16).astype(jnp.float32) * weight_grad
            for weight, weight_grad in zip(weights, weight_grads)
        ]
        delta = jnp.sum(mixed[0] + mixed[1] + mixed[2], axis=0, keepdims=True)
        result = None
        for side in range(3):
            score_grad = (weights[side] * (weight_grads[side] - delta)).astype(jnp.bfloat16)
            term = tn(score_grad, both(key_refs[2 * side], key_refs[2 * side + 1], head, 0))
            result = term if result is None else result + term
        result = (result * scale).astype(jnp.bfloat16)
        dq_k[head] = result[:block]
        dq_o[head] = result[block:]
        stats[head, 0:1, :] = peak + jnp.log2(total)
        stats[head, 1:2, :] = delta


def key_kernel(factor, scale, heads, offset, table, kv_k, kv_o, qd_k, qd_o, side_a, side_b, *refs):
    stat_refs, (dkv_k, dkv_o) = refs[:3], refs[3:]
    block = kv_k.shape[2]
    first = pl.program_id(0) * heads + offset
    for head in range(heads):
        keys = both(kv_k, kv_o, head, 0)
        values = both(kv_k, kv_o, head, 1)
        key_grad = None
        value_grad = None
        for side in range(3):
            if side == 0:
                queries, grads = both(qd_k, qd_o, head, 0), both(qd_k, qd_o, head, 1)
            else:
                ref = (side_a, side_b)[side - 1]
                queries = jnp.concatenate([ref[head, 0], ref[head, 2]], axis=0)
                grads = jnp.concatenate([ref[head, 1], ref[head, 3]], axis=0)
            at = (first + head) * 24 + side * 8 + 4
            biases = [[table[at + 2 * a + b] for b in range(2)] for a in range(2)]
            level = stat_refs[side][head, 0:1, :]
            delta = stat_refs[side][head, 1:2, :]
            weights = jnp.exp2(biased(nt(keys, queries) * factor, biases, block) - level)
            weight_grad = nt(values, grads)
            score_grad = (weights * (weight_grad - delta)).astype(jnp.bfloat16)
            value_term = nn(weights.astype(jnp.bfloat16), grads)
            key_term = nn(score_grad, queries)
            value_grad = value_term if value_grad is None else value_grad + value_term
            key_grad = key_term if key_grad is None else key_grad + key_term
        key_grad = (key_grad * scale).astype(jnp.bfloat16)
        value_grad = value_grad.astype(jnp.bfloat16)
        dkv_k[head, 0] = key_grad[:block]
        dkv_o[head, 0] = key_grad[block:]
        dkv_k[head, 1] = value_grad[:block]
        dkv_o[head, 1] = value_grad[block:]


def bias_table(block_mask, heads, range_index, position, range_total):
    reach = (block_mask.shape[2] - 1) // 2
    even = range_index % 2 == 0
    ranges = jnp.stack(
        [range_index, range_index ^ 1, jnp.where(even, range_index - 1, range_index + 1)]
    )
    slots = jnp.stack([position, 1 - position])
    mine = range_index * RANGE + slots
    others = ranges[:, None] * RANGE + slots[None, :]
    shape = (3, 2, 2)
    key_first = jnp.broadcast_to(others[:, :, None], shape)
    query_first = jnp.broadcast_to(mine[None, None, :], shape)
    key_second = jnp.broadcast_to(mine[None, :, None], shape)
    query_second = jnp.broadcast_to(others[:, None, :], shape)
    key = jnp.stack([key_first, key_second], axis=1)
    query = jnp.stack([query_first, query_second], axis=1)
    total = range_total * RANGE
    inside = (key >= 0) & (key < total) & (query >= 0) & (query < total) & (abs(key - query) <= reach)
    picked = jax.nn.one_hot(query.reshape(-1), total, dtype=jnp.int32)[:, :, None] * (
        jax.nn.one_hot((key - query + reach).reshape(-1), 2 * reach + 1, dtype=jnp.int32)[:, None, :]
    )
    own = lax.dynamic_slice_in_dim(block_mask, position * heads, heads)
    found = jnp.sum(own[:, None] * picked[None], axis=(2, 3))
    allowed = (found > 0) & inside.reshape(-1)[None]
    return jnp.where(allowed, 0.0, NEVER).astype(jnp.float32).reshape(-1)


def per_device(queries, keys, values, out_grad, block_mask):
    block, head_count, width = queries.shape
    local = head_count // RANGE
    scale = 1.0 / math.sqrt(width)
    factor = scale * math.log2(math.e)
    device = lax.axis_index("seq")
    position = device % RANGE
    range_total = lax.axis_size("seq") // RANGE

    def by_head(left, right):
        return jnp.stack([jnp.transpose(left, (1, 0, 2)), jnp.transpose(right, (1, 0, 2))], axis=1)

    def half(pair, place):
        return lax.dynamic_slice_in_dim(pair, place * local, local)

    kv, qd = by_head(keys, values), by_head(queries, out_grad)
    kv_send = half(kv, 1 - position)
    kv_keep = half(after(kv, kv_send), position)
    qd_send, qd_keep = half(qd, 1 - position), half(qd, position)
    kv_other = across(kv_send, "seq")
    kv_sides = [beside(kv_keep, 0), beside(kv_keep, 1)]
    qd_other = across(after(qd_send, kv_other), "seq")
    kv_sides_other = [beside(kv_other, 0), beside(kv_other, 1)]
    cuts = cut_heads(local)
    qd_pieces = [
        jnp.concatenate([qd_keep[low:high], qd_other[low:high]], axis=1) for low, high in zip(cuts, cuts[1:])
    ]
    qd_sides = [[beside(qd_pieces[0], 0), beside(qd_pieces[0], 1)]]
    table = bias_table(block_mask, local, device // RANGE, position, range_total)

    heads = 2 if local % 2 == 0 else 1
    pair_spec = pl.BlockSpec((heads, 2, block, width), lambda i: (i, 0, 0, 0))
    quad_spec = pl.BlockSpec((heads, 4, block, width), lambda i: (i, 0, 0, 0))
    one_spec = pl.BlockSpec((heads, block, width), lambda i: (i, 0, 0))
    stat_spec = pl.BlockSpec((heads, 2, 2 * block), lambda i: (i, 0, 0))
    table_spec = pl.BlockSpec(memory_space=pltpu.SMEM)
    params = pltpu.CompilerParams(vmem_limit_bytes=VMEM_BYTES)
    tile = 4 * block * block * width

    dq_keep, dq_send, stats = pl.pallas_call(
        partial(query_kernel, factor, scale, heads),
        grid=(local // heads,),
        in_specs=[table_spec] + [pair_spec] * 8,
        out_specs=[one_spec, one_spec, stat_spec],
        out_shape=[
            jax.ShapeDtypeStruct((local, block, width), jnp.bfloat16),
            jax.ShapeDtypeStruct((local, block, width), jnp.bfloat16),
            jax.ShapeDtypeStruct((local, 2, 2 * block), jnp.float32),
        ],
        compiler_params=params,
        cost_estimate=pl.CostEstimate(
            flops=WORK * 2 * 9 * local * tile, bytes_accessed=20 * local * block * width * 2, transcendentals=0
        ),
    )(
        table,
        qd_keep,
        qd_other,
        kv_keep,
        kv_other,
        kv_sides[0],
        kv_sides_other[0],
        kv_sides[1],
        kv_sides_other[1],
    )
    stats = after(stats, qd_sides[0][0])
    stat_sides = [beside(stats, 0), beside(stats, 1)]
    dq_back = across(dq_send, "seq")
    dkv_keep, dkv_back = [], []
    for index, (low, high) in enumerate(zip(cuts, cuts[1:])):
        arrived = qd_sides[index]
        if index + 1 < len(qd_pieces):
            piece = after(qd_pieces[index + 1], qd_sides[-1][0] if index == 0 else dkv_back[0])
            qd_sides.append([beside(piece, 0), beside(piece, 1)])
        count = high - low
        heads = count
        shift = low // heads
        pair_spec = pl.BlockSpec((heads, 2, block, width), lambda i: (i, 0, 0, 0))
        quad_spec = pl.BlockSpec((heads, 4, block, width), lambda i: (i, 0, 0, 0))
        part_spec = pl.BlockSpec((heads, 2, block, width), lambda i, shift=shift: (i + shift, 0, 0, 0))
        stat_part = pl.BlockSpec((heads, 2, 2 * block), lambda i, shift=shift: (i + shift, 0, 0))
        keep, send = pl.pallas_call(
            partial(key_kernel, factor, scale, heads, low),
            grid=(count // heads,),
            in_specs=[table_spec] + [part_spec] * 4 + [quad_spec] * 2 + [stat_part] * 3,
            out_specs=[pair_spec, pair_spec],
            out_shape=[jax.ShapeDtypeStruct((count, 2, block, width), jnp.bfloat16)] * 2,
            compiler_params=params,
            cost_estimate=pl.CostEstimate(
                flops=WORK * 2 * 12 * count * tile, bytes_accessed=20 * count * block * width * 2, transcendentals=0
            ),
        )(
            table,
            kv_keep,
            kv_other,
            qd_keep,
            qd_other,
            *arrived,
            stats,
            *stat_sides,
        )
        dkv_keep.append(keep)
        dkv_back.append(across(send, "seq"))
    dkv_keep = jnp.concatenate(dkv_keep, axis=0)
    dkv_back = jnp.concatenate(dkv_back, axis=0)

    def home(mine, returned):
        low = jnp.where(position == 0, mine, returned)
        high = jnp.where(position == 0, returned, mine)
        return jnp.transpose(jnp.concatenate([low, high], axis=0), (1, 0, 2))

    return (
        home(dq_keep, dq_back),
        home(dkv_keep[:, 0], dkv_back[:, 0]),
        home(dkv_keep[:, 1], dkv_back[:, 1]),
    )


def solution(mesh):
    rows = P(("dp", "seq"), None, None)
    return jax.shard_map(
        per_device,
        mesh=mesh,
        in_specs=(rows, rows, rows, rows, P()),
        out_specs=(rows, rows, rows),
        check_vma=False,
    )
```

```python
from functools import partial
import math

import jax
import jax.numpy as jnp
from jax import lax
from jax.experimental import pallas as pl
from jax.experimental.pallas import tpu as pltpu
from jax.sharding import PartitionSpec as P

RANGE = 2
NEVER = -1e30
WORK = 8
VMEM_BYTES = 40 * 2**20


def cut_heads(local):
    step = (2 * local // 5 + 1) // 2 * 2
    return sorted({0, min(step, local), min(2 * step, local), local})


def across(value, axis):
    size = lax.axis_size(axis)
    return lax.ppermute(value, axis, [(i, i ^ 1) for i in range(size)])


def after(value, *earlier):
    return lax.optimization_barrier((value, *earlier))[0]


def partner_of(index, kind, range_total):
    other = index ^ 1 if kind == 0 else (index - 1 if index % 2 == 0 else index + 1)
    return other if 0 <= other < range_total else None


def beside(value, kind):
    size, clips = lax.axis_size("seq"), lax.axis_size("dp")
    pairs = []
    for i in range(size):
        other = partner_of(i // RANGE, kind, size // RANGE)
        for clip in range(clips):
            if other is not None:
                pairs.append((i * clips + clip, (other * RANGE + i % RANGE) * clips + clip))
            elif clips % 2 == 0:
                pairs.append((i * clips + clip, i * clips + (clip ^ 1)))
    return lax.ppermute(value, ("seq", "dp"), pairs)


def nt(left, right):
    return lax.dot_general(left, right, (((1,), (1,)), ((), ())), preferred_element_type=jnp.float32)


def nn(left, right):
    return lax.dot_general(left, right, (((1,), (0,)), ((), ())), preferred_element_type=jnp.float32)


def tn(left, right):
    return lax.dot_general(left, right, (((0,), (0,)), ((), ())), preferred_element_type=jnp.float32)


def both(keep, other, head, which):
    return jnp.concatenate([keep[head, which], other[head, which]], axis=0)


def biased(scores, biases, block):
    rows = []
    for a in range(2):
        rows.append(
            jnp.concatenate(
                [
                    scores[a * block : (a + 1) * block, b * block : (b + 1) * block] + biases[a][b]
                    for b in range(2)
                ],
                axis=1,
            )
        )
    return jnp.concatenate(rows, axis=0)


def query_kernel(factor, scale, heads, table, qd_k, qd_o, *refs):
    key_refs, (dq_k, dq_o, stats) = refs[:6], refs[6:]
    block = qd_k.shape[2]
    first = pl.program_id(0) * heads
    for head in range(heads):
        queries = both(qd_k, qd_o, head, 0)
        grads = both(qd_k, qd_o, head, 1)
        scores = []
        for side in range(3):
            keys = both(key_refs[2 * side], key_refs[2 * side + 1], head, 0)
            at = (first + head) * 24 + side * 8
            biases = [[table[at + 2 * a + b] for b in range(2)] for a in range(2)]
            scores.append(biased(nt(keys, queries) * factor, biases, block))
        peak = jnp.max(jnp.maximum(jnp.maximum(scores[0], scores[1]), scores[2]), axis=0, keepdims=True)
        exps = [jnp.exp2(element - peak) for element in scores]
        total = jnp.sum(exps[0] + exps[1] + exps[2], axis=0, keepdims=True)
        weight_grads = [
            nt(both(key_refs[2 * side], key_refs[2 * side + 1], head, 1), grads) for side in range(3)
        ]
        inverse = 1.0 / total
        weights = [element * inverse for element in exps]
        mixed = [
            weight.astype(jnp.bfloat16).astype(jnp.float32) * weight_grad
            for weight, weight_grad in zip(weights, weight_grads)
        ]
        delta = jnp.sum(mixed[0] + mixed[1] + mixed[2], axis=0, keepdims=True)
        result = None
        for side in range(3):
            score_grad = (weights[side] * (weight_grads[side] - delta)).astype(jnp.bfloat16)
            term = tn(score_grad, both(key_refs[2 * side], key_refs[2 * side + 1], head, 0))
            result = term if result is None else result + term
        result = (result * scale).astype(jnp.bfloat16)
        dq_k[head] = result[:block]
        dq_o[head] = result[block:]
        stats[head, 0:1, :] = peak + jnp.log2(total)
        stats[head, 1:2, :] = delta


def key_kernel(factor, scale, heads, offset, table, kv_k, kv_o, qd_k, qd_o, side_a, side_b, *refs):
    stat_refs, (dkv_k, dkv_o) = refs[:3], refs[3:]
    block = kv_k.shape[2]
    first = pl.program_id(0) * heads + offset
    for head in range(heads):
        keys = both(kv_k, kv_o, head, 0)
        values = both(kv_k, kv_o, head, 1)
        key_grad = None
        value_grad = None
        for side in range(3):
            if side == 0:
                queries, grads = both(qd_k, qd_o, head, 0), both(qd_k, qd_o, head, 1)
            else:
                ref = (side_a, side_b)[side - 1]
                queries = jnp.concatenate([ref[head, 0], ref[head, 2]], axis=0)
                grads = jnp.concatenate([ref[head, 1], ref[head, 3]], axis=0)
            at = (first + head) * 24 + side * 8 + 4
            biases = [[table[at + 2 * a + b] for b in range(2)] for a in range(2)]
            level = stat_refs[side][head, 0:1, :]
            delta = stat_refs[side][head, 1:2, :]
            raw = nt(keys, queries) * factor
            halves = []
            for a in range(2):
                shift = jnp.concatenate(
                    [biases[a][b] - level[:, b * block : (b + 1) * block] for b in range(2)], axis=1
                )
                halves.append(raw[a * block : (a + 1) * block] + shift)
            weights = jnp.exp2(jnp.concatenate(halves, axis=0))
            weight_grad = nt(values, grads)
            score_grad = (weights * (weight_grad - delta)).astype(jnp.bfloat16)
            value_term = nn(weights.astype(jnp.bfloat16), grads)
            key_term = nn(score_grad, queries)
            value_grad = value_term if value_grad is None else value_grad + value_term
            key_grad = key_term if key_grad is None else key_grad + key_term
        key_grad = (key_grad * scale).astype(jnp.bfloat16)
        value_grad = value_grad.astype(jnp.bfloat16)
        dkv_k[head, 0] = key_grad[:block]
        dkv_o[head, 0] = key_grad[block:]
        dkv_k[head, 1] = value_grad[:block]
        dkv_o[head, 1] = value_grad[block:]


def bias_table(block_mask, heads, range_index, position, range_total):
    reach = (block_mask.shape[2] - 1) // 2
    even = range_index % 2 == 0
    ranges = jnp.stack(
        [range_index, range_index ^ 1, jnp.where(even, range_index - 1, range_index + 1)]
    )
    slots = jnp.stack([position, 1 - position])
    mine = range_index * RANGE + slots
    others = ranges[:, None] * RANGE + slots[None, :]
    shape = (3, 2, 2)
    key_first = jnp.broadcast_to(others[:, :, None], shape)
    query_first = jnp.broadcast_to(mine[None, None, :], shape)
    key_second = jnp.broadcast_to(mine[None, :, None], shape)
    query_second = jnp.broadcast_to(others[:, None, :], shape)
    key = jnp.stack([key_first, key_second], axis=1)
    query = jnp.stack([query_first, query_second], axis=1)
    total = range_total * RANGE
    inside = (key >= 0) & (key < total) & (query >= 0) & (query < total) & (abs(key - query) <= reach)
    picked = jax.nn.one_hot(query.reshape(-1), total, dtype=jnp.int32)[:, :, None] * (
        jax.nn.one_hot((key - query + reach).reshape(-1), 2 * reach + 1, dtype=jnp.int32)[:, None, :]
    )
    own = lax.dynamic_slice_in_dim(block_mask, position * heads, heads)
    found = jnp.sum(own[:, None] * picked[None], axis=(2, 3))
    allowed = (found > 0) & inside.reshape(-1)[None]
    return jnp.where(allowed, 0.0, NEVER).astype(jnp.float32).reshape(-1)


def per_device(queries, keys, values, out_grad, block_mask):
    block, head_count, width = queries.shape
    local = head_count // RANGE
    scale = 1.0 / math.sqrt(width)
    factor = scale * math.log2(math.e)
    device = lax.axis_index("seq")
    position = device % RANGE
    range_total = lax.axis_size("seq") // RANGE

    def by_head(left, right):
        return jnp.stack([jnp.transpose(left, (1, 0, 2)), jnp.transpose(right, (1, 0, 2))], axis=1)

    def half(pair, place):
        return lax.dynamic_slice_in_dim(pair, place * local, local)

    kv, qd = by_head(keys, values), by_head(queries, out_grad)
    kv_send = half(kv, 1 - position)
    kv_keep = half(after(kv, kv_send), position)
    qd_send, qd_keep = half(qd, 1 - position), half(qd, position)
    kv_other = across(kv_send, "seq")
    kv_sides = [beside(kv_keep, 0), beside(kv_keep, 1)]
    qd_other = across(after(qd_send, kv_other), "seq")
    kv_sides_other = [beside(kv_other, 0), beside(kv_other, 1)]
    cuts = cut_heads(local)
    qd_pieces = [
        jnp.concatenate([qd_keep[low:high], qd_other[low:high]], axis=1) for low, high in zip(cuts, cuts[1:])
    ]
    qd_sides = [[beside(qd_pieces[0], 0), beside(qd_pieces[0], 1)]]
    table = bias_table(block_mask, local, device // RANGE, position, range_total)

    heads = local // 2 if local % 2 == 0 else local
    pair_spec = pl.BlockSpec((heads, 2, block, width), lambda i: (i, 0, 0, 0))
    quad_spec = pl.BlockSpec((heads, 4, block, width), lambda i: (i, 0, 0, 0))
    one_spec = pl.BlockSpec((heads, block, width), lambda i: (i, 0, 0))
    stat_spec = pl.BlockSpec((heads, 2, 2 * block), lambda i: (i, 0, 0))
    table_spec = pl.BlockSpec(memory_space=pltpu.SMEM)
    params = pltpu.CompilerParams(vmem_limit_bytes=VMEM_BYTES)
    tile = 4 * block * block * width

    dq_keep, dq_send, stats = pl.pallas_call(
        partial(query_kernel, factor, scale, heads),
        grid=(local // heads,),
        in_specs=[table_spec] + [pair_spec] * 8,
        out_specs=[one_spec, one_spec, stat_spec],
        out_shape=[
            jax.ShapeDtypeStruct((local, block, width), jnp.bfloat16),
            jax.ShapeDtypeStruct((local, block, width), jnp.bfloat16),
            jax.ShapeDtypeStruct((local, 2, 2 * block), jnp.float32),
        ],
        compiler_params=params,
        cost_estimate=pl.CostEstimate(
            flops=2 * WORK * 2 * 9 * local * tile, bytes_accessed=20 * local * block * width * 2, transcendentals=0
        ),
    )(
        table,
        qd_keep,
        qd_other,
        kv_keep,
        kv_other,
        kv_sides[0],
        kv_sides_other[0],
        kv_sides[1],
        kv_sides_other[1],
    )
    stats = after(stats, qd_sides[0][0])
    stat_sides = [beside(stats, 0), beside(stats, 1)]
    dq_back = across(dq_send, "seq")
    dkv_keep, dkv_back = [], []
    for index, (low, high) in enumerate(zip(cuts, cuts[1:])):
        arrived = qd_sides[index]
        if index + 1 < len(qd_pieces):
            piece = after(qd_pieces[index + 1], qd_sides[-1][0] if index == 0 else dkv_back[0])
            qd_sides.append([beside(piece, 0), beside(piece, 1)])
        count = high - low
        heads = count
        shift = low // heads
        pair_spec = pl.BlockSpec((heads, 2, block, width), lambda i: (i, 0, 0, 0))
        quad_spec = pl.BlockSpec((heads, 4, block, width), lambda i: (i, 0, 0, 0))
        part_spec = pl.BlockSpec((heads, 2, block, width), lambda i, shift=shift: (i + shift, 0, 0, 0))
        stat_part = pl.BlockSpec((heads, 2, 2 * block), lambda i, shift=shift: (i + shift, 0, 0))
        keep, send = pl.pallas_call(
            partial(key_kernel, factor, scale, heads, low),
            grid=(count // heads,),
            in_specs=[table_spec] + [part_spec] * 4 + [quad_spec] * 2 + [stat_part] * 3,
            out_specs=[pair_spec, pair_spec],
            out_shape=[jax.ShapeDtypeStruct((count, 2, block, width), jnp.bfloat16)] * 2,
            compiler_params=params,
            cost_estimate=pl.CostEstimate(
                flops=WORK * 2 * 12 * count * tile, bytes_accessed=20 * count * block * width * 2, transcendentals=0
            ),
        )(
            table,
            kv_keep,
            kv_other,
            qd_keep,
            qd_other,
            *arrived,
            stats,
            *stat_sides,
        )
        dkv_keep.append(keep)
        dkv_back.append(across(send, "seq"))
    dkv_keep = jnp.concatenate(dkv_keep, axis=0)
    dkv_back = jnp.concatenate(dkv_back, axis=0)

    def home(mine, returned):
        low = jnp.where(position == 0, mine, returned)
        high = jnp.where(position == 0, returned, mine)
        return jnp.transpose(jnp.concatenate([low, high], axis=0), (1, 0, 2))

    return (
        home(dq_keep, dq_back),
        home(dkv_keep[:, 0], dkv_back[:, 0]),
        home(dkv_keep[:, 1], dkv_back[:, 1]),
    )


def solution(mesh):
    rows = P(("dp", "seq"), None, None)
    return jax.shard_map(
        per_device,
        mesh=mesh,
        in_specs=(rows, rows, rows, rows, P()),
        out_specs=(rows, rows, rows),
        check_vma=False,
    )
```

```python
from functools import partial
import math

import jax
import jax.numpy as jnp
from jax import lax
from jax.experimental import pallas as pl
from jax.experimental.pallas import tpu as pltpu
from jax.sharding import PartitionSpec as P

RANGE = 2
NEVER = -1e30
WORK = 8
VMEM_BYTES = 40 * 2**20


def cut_heads(local):
    step = (2 * local // 5 + 1) // 2 * 2
    return sorted({0, min(step, local), min(2 * step, local), local})


def across(value, axis):
    size = lax.axis_size(axis)
    return lax.ppermute(value, axis, [(i, i ^ 1) for i in range(size)])


def after(value, *earlier):
    return lax.optimization_barrier((value, *earlier))[0]


def partner_of(index, kind, range_total):
    other = index ^ 1 if kind == 0 else (index - 1 if index % 2 == 0 else index + 1)
    return other if 0 <= other < range_total else None


def beside(value, kind):
    size, clips = lax.axis_size("seq"), lax.axis_size("dp")
    pairs = []
    for i in range(size):
        other = partner_of(i // RANGE, kind, size // RANGE)
        for clip in range(clips):
            if other is not None:
                pairs.append((i * clips + clip, (other * RANGE + i % RANGE) * clips + clip))
            elif clips % 2 == 0:
                pairs.append((i * clips + clip, i * clips + (clip ^ 1)))
    return lax.ppermute(value, ("seq", "dp"), pairs)


def nt(left, right):
    return lax.dot_general(left, right, (((1,), (1,)), ((), ())), preferred_element_type=jnp.float32)


def nn(left, right):
    return lax.dot_general(left, right, (((1,), (0,)), ((), ())), preferred_element_type=jnp.float32)


def tn(left, right):
    return lax.dot_general(left, right, (((0,), (0,)), ((), ())), preferred_element_type=jnp.float32)


def both(keep, other, head, which):
    return jnp.concatenate([keep[head, which], other[head, which]], axis=0)


def biased(scores, biases, block):
    rows = []
    for a in range(2):
        rows.append(
            jnp.concatenate(
                [
                    scores[a * block : (a + 1) * block, b * block : (b + 1) * block] + biases[a][b]
                    for b in range(2)
                ],
                axis=1,
            )
        )
    return jnp.concatenate(rows, axis=0)


def query_kernel(factor, scale, heads, table, qd_k, qd_o, *refs):
    key_refs, (dq_k, dq_o, stats) = refs[:6], refs[6:]
    block = qd_k.shape[2]
    first = pl.program_id(0) * heads
    for head in range(heads):
        queries = both(qd_k, qd_o, head, 0)
        grads = both(qd_k, qd_o, head, 1)
        scores = []
        for side in range(3):
            keys = both(key_refs[2 * side], key_refs[2 * side + 1], head, 0)
            at = (first + head) * 24 + side * 8
            biases = [[table[at + 2 * a + b] for b in range(2)] for a in range(2)]
            scores.append(biased(nt(keys, queries) * factor, biases, block))
        peak = jnp.max(jnp.maximum(jnp.maximum(scores[0], scores[1]), scores[2]), axis=0, keepdims=True)
        exps = [jnp.exp2(element - peak) for element in scores]
        total = jnp.sum(exps[0] + exps[1] + exps[2], axis=0, keepdims=True)
        weight_grads = [
            nt(both(key_refs[2 * side], key_refs[2 * side + 1], head, 1), grads) for side in range(3)
        ]
        inverse = 1.0 / total
        weights = [element * inverse for element in exps]
        mixed = [
            weight.astype(jnp.bfloat16).astype(jnp.float32) * weight_grad
            for weight, weight_grad in zip(weights, weight_grads)
        ]
        delta = jnp.sum(mixed[0] + mixed[1] + mixed[2], axis=0, keepdims=True)
        result = None
        for side in range(3):
            score_grad = (weights[side] * (weight_grads[side] - delta)).astype(jnp.bfloat16)
            term = tn(score_grad, both(key_refs[2 * side], key_refs[2 * side + 1], head, 0))
            result = term if result is None else result + term
        result = (result * scale).astype(jnp.bfloat16)
        dq_k[head] = result[:block]
        dq_o[head] = result[block:]
        stats[head, 0:1, :] = peak + jnp.log2(total)
        stats[head, 1:2, :] = delta


def key_kernel(factor, scale, heads, offset, table, kv_k, kv_o, qd_k, qd_o, side_a, side_b, *refs):
    stat_refs, (dkv_k, dkv_o) = refs[:3], refs[3:]
    block = kv_k.shape[2]
    first = pl.program_id(0) * heads + offset
    for head in range(heads):
        keys = both(kv_k, kv_o, head, 0)
        values = both(kv_k, kv_o, head, 1)
        key_grad = None
        value_grad = None
        for side in range(3):
            if side == 0:
                queries, grads = both(qd_k, qd_o, head, 0), both(qd_k, qd_o, head, 1)
            else:
                ref = (side_a, side_b)[side - 1]
                queries = jnp.concatenate([ref[head, 0], ref[head, 2]], axis=0)
                grads = jnp.concatenate([ref[head, 1], ref[head, 3]], axis=0)
            at = (first + head) * 24 + side * 8 + 4
            biases = [[table[at + 2 * a + b] for b in range(2)] for a in range(2)]
            level = stat_refs[side][head, 0:1, :]
            delta = stat_refs[side][head, 1:2, :]
            raw = nt(keys, queries) * factor
            halves = []
            for a in range(2):
                shift = jnp.concatenate(
                    [biases[a][b] - level[:, b * block : (b + 1) * block] for b in range(2)], axis=1
                )
                halves.append(raw[a * block : (a + 1) * block] + shift)
            weights = jnp.exp2(jnp.concatenate(halves, axis=0))
            weight_grad = nt(values, grads)
            score_grad = (weights * (weight_grad - delta)).astype(jnp.bfloat16)
            value_term = nn(weights.astype(jnp.bfloat16), grads)
            key_term = nn(score_grad, queries)
            value_grad = value_term if value_grad is None else value_grad + value_term
            key_grad = key_term if key_grad is None else key_grad + key_term
        key_grad = (key_grad * scale).astype(jnp.bfloat16)
        value_grad = value_grad.astype(jnp.bfloat16)
        dkv_k[head, 0] = key_grad[:block]
        dkv_o[head, 0] = key_grad[block:]
        dkv_k[head, 1] = value_grad[:block]
        dkv_o[head, 1] = value_grad[block:]


def bias_table(block_mask, heads, range_index, position, range_total):
    reach = (block_mask.shape[2] - 1) // 2
    even = range_index % 2 == 0
    ranges = jnp.stack(
        [range_index, range_index ^ 1, jnp.where(even, range_index - 1, range_index + 1)]
    )
    slots = jnp.stack([position, 1 - position])
    mine = range_index * RANGE + slots
    others = ranges[:, None] * RANGE + slots[None, :]
    shape = (3, 2, 2)
    key_first = jnp.broadcast_to(others[:, :, None], shape)
    query_first = jnp.broadcast_to(mine[None, None, :], shape)
    key_second = jnp.broadcast_to(mine[None, :, None], shape)
    query_second = jnp.broadcast_to(others[:, None, :], shape)
    key = jnp.stack([key_first, key_second], axis=1)
    query = jnp.stack([query_first, query_second], axis=1)
    total = range_total * RANGE
    inside = (key >= 0) & (key < total) & (query >= 0) & (query < total) & (abs(key - query) <= reach)
    picked = jax.nn.one_hot(query.reshape(-1), total, dtype=jnp.int32)[:, :, None] * (
        jax.nn.one_hot((key - query + reach).reshape(-1), 2 * reach + 1, dtype=jnp.int32)[:, None, :]
    )
    own = lax.dynamic_slice_in_dim(block_mask, position * heads, heads)
    found = jnp.sum(own[:, None] * picked[None], axis=(2, 3))
    allowed = (found > 0) & inside.reshape(-1)[None]
    return jnp.where(allowed, 0.0, NEVER).astype(jnp.float32).reshape(-1)


def per_device(queries, keys, values, out_grad, block_mask):
    block, head_count, width = queries.shape
    local = head_count // RANGE
    scale = 1.0 / math.sqrt(width)
    factor = scale * math.log2(math.e)
    device = lax.axis_index("seq")
    position = device % RANGE
    range_total = lax.axis_size("seq") // RANGE

    def by_head(left, right):
        return jnp.stack([jnp.transpose(left, (1, 0, 2)), jnp.transpose(right, (1, 0, 2))], axis=1)

    def half(pair, place):
        return lax.dynamic_slice_in_dim(pair, place * local, local)

    kv, qd = by_head(keys, values), by_head(queries, out_grad)
    def cut(array, place):
        return half(jnp.transpose(array, (1, 0, 2)), place)

    kv_send = jnp.stack([cut(keys, 1 - position), cut(values, 1 - position)], axis=1)
    later = after(position, kv_send)
    kv_keep = jnp.stack([cut(keys, later), cut(values, later)], axis=1)
    qd_send, qd_keep = half(qd, 1 - position), half(qd, position)
    kv_other = across(kv_send, "seq")
    kv_sides = [beside(kv_keep, 0), beside(kv_keep, 1)]
    qd_other = across(after(qd_send, kv_other), "seq")
    kv_sides_other = [beside(kv_other, 0), beside(kv_other, 1)]
    cuts = cut_heads(local)
    qd_pieces = [
        jnp.concatenate([qd_keep[low:high], qd_other[low:high]], axis=1) for low, high in zip(cuts, cuts[1:])
    ]
    qd_sides = [[beside(qd_pieces[0], 0), beside(qd_pieces[0], 1)]]
    table = bias_table(block_mask, local, device // RANGE, position, range_total)

    heads = local // 2 if local % 2 == 0 else local
    pair_spec = pl.BlockSpec((heads, 2, block, width), lambda i: (i, 0, 0, 0))
    quad_spec = pl.BlockSpec((heads, 4, block, width), lambda i: (i, 0, 0, 0))
    one_spec = pl.BlockSpec((heads, block, width), lambda i: (i, 0, 0))
    stat_spec = pl.BlockSpec((heads, 2, 2 * block), lambda i: (i, 0, 0))
    table_spec = pl.BlockSpec(memory_space=pltpu.SMEM)
    params = pltpu.CompilerParams(vmem_limit_bytes=VMEM_BYTES)
    tile = 4 * block * block * width

    dq_keep, dq_send, stats = pl.pallas_call(
        partial(query_kernel, factor, scale, heads),
        grid=(local // heads,),
        in_specs=[table_spec] + [pair_spec] * 8,
        out_specs=[one_spec, one_spec, stat_spec],
        out_shape=[
            jax.ShapeDtypeStruct((local, block, width), jnp.bfloat16),
            jax.ShapeDtypeStruct((local, block, width), jnp.bfloat16),
            jax.ShapeDtypeStruct((local, 2, 2 * block), jnp.float32),
        ],
        compiler_params=params,
        cost_estimate=pl.CostEstimate(
            flops=2 * WORK * 2 * 9 * local * tile, bytes_accessed=20 * local * block * width * 2, transcendentals=0
        ),
    )(
        table,
        qd_keep,
        qd_other,
        kv_keep,
        kv_other,
        kv_sides[0],
        kv_sides_other[0],
        kv_sides[1],
        kv_sides_other[1],
    )
    stats = after(stats, qd_sides[0][0])
    stat_sides = [beside(stats, 0), beside(stats, 1)]
    dq_back = across(dq_send, "seq")
    dkv_keep, dkv_back = [], []
    for index, (low, high) in enumerate(zip(cuts, cuts[1:])):
        arrived = qd_sides[index]
        if index + 1 < len(qd_pieces):
            piece = after(qd_pieces[index + 1], qd_sides[-1][0] if index == 0 else dkv_back[0])
            qd_sides.append([beside(piece, 0), beside(piece, 1)])
        count = high - low
        heads = count
        shift = low // heads
        pair_spec = pl.BlockSpec((heads, 2, block, width), lambda i: (i, 0, 0, 0))
        quad_spec = pl.BlockSpec((heads, 4, block, width), lambda i: (i, 0, 0, 0))
        part_spec = pl.BlockSpec((heads, 2, block, width), lambda i, shift=shift: (i + shift, 0, 0, 0))
        stat_part = pl.BlockSpec((heads, 2, 2 * block), lambda i, shift=shift: (i + shift, 0, 0))
        keep, send = pl.pallas_call(
            partial(key_kernel, factor, scale, heads, low),
            grid=(count // heads,),
            in_specs=[table_spec] + [part_spec] * 4 + [quad_spec] * 2 + [stat_part] * 3,
            out_specs=[pair_spec, pair_spec],
            out_shape=[jax.ShapeDtypeStruct((count, 2, block, width), jnp.bfloat16)] * 2,
            compiler_params=params,
            cost_estimate=pl.CostEstimate(
                flops=WORK * 2 * 12 * count * tile, bytes_accessed=20 * count * block * width * 2, transcendentals=0
            ),
        )(
            table,
            kv_keep,
            kv_other,
            qd_keep,
            qd_other,
            *arrived,
            stats,
            *stat_sides,
        )
        dkv_keep.append(keep)
        dkv_back.append(across(send, "seq"))
    dkv_keep = jnp.concatenate(dkv_keep, axis=0)
    dkv_back = jnp.concatenate(dkv_back, axis=0)

    def home(mine, returned):
        low = jnp.where(position == 0, mine, returned)
        high = jnp.where(position == 0, returned, mine)
        return jnp.transpose(jnp.concatenate([low, high], axis=0), (1, 0, 2))

    return (
        home(dq_keep, dq_back),
        home(dkv_keep[:, 0], dkv_back[:, 0]),
        home(dkv_keep[:, 1], dkv_back[:, 1]),
    )


def solution(mesh):
    rows = P(("dp", "seq"), None, None)
    return jax.shard_map(
        per_device,
        mesh=mesh,
        in_specs=(rows, rows, rows, rows, P()),
        out_specs=(rows, rows, rows),
        check_vma=False,
    )
```
